256 devices in a mesh: role: 4 (over x), dp: 8 (over z_hi, core), seq: 8 (over y, z_lo).
Axes of the slice: x: 4, y: 4, z: 8 (z_hi: 4, z_lo: 2; z = z_hi * 2 + z_lo), core: 2. Of those that a mesh axis runs over, the one named last changes fastest.
Arguments:
- latents: bfloat16 [8192, 5120], P(('dp', 'seq'), 'role'), may hold values from -6 to 6
- noise: bfloat16 [8192, 5120], P(('dp', 'seq'), 'role'), may hold values from -6 to 6
- timesteps: int32 [8], P('dp'), may hold values from 0 to 999
- qkv_weight: bfloat16 [5120, 4, 8, 3, 256], P('dp', 'role', 'seq'), may hold values from -0.078125 to 0.078125
- qk_gain: float32 [2, 2, 128], replicated, may hold values from 0.5 to 1.5
- fake_cotangent: bfloat16 [8192, 2, 8, 256], P('dp', None, 'seq'), may hold values from -6 to 6
Outputs:
- dmd_grad: bfloat16 [8192, 4096], P(('dp', 'seq'), 'role')
- value_grad: float32 [4, 2560, 8, 256], P('role', 'dp', 'seq')
The draws below stay inside these ranges and needn't reach their ends.
All inputs are finite; a program needn't handle non-finite values. Where the reference program divides by a largest or mean magnitude, that divisor is 1e-20 or more.
Results may differ from the reference program's by a relative error of at most 0.018.
Values may be sent and summed in bfloat16 or wider, within the bound.
No kernel may reach another device: no remote copies, remote signals or barrier semaphores. Data moves between devices by JAX's collectives and lax.ppermute only.
A program may use at most 128 MiB of HBM per device.

```python
import math
import jax
import jax.numpy as jnp
from jax import lax

D = 5120
HDIM = 128
HQ = 1
TOK_DEV = 128
STEPS = 1000
CLIPS = 8
TOKENS = 8192
N_DP = 8
N_SEQ = 8


def plant(entries, own_key, least, top_value):
    index_at = [jax.random.randint(jax.random.fold_in(own_key, axis), (), 0, length) for axis, length in enumerate(entries.shape)]
    main_axis = entries.shape.index(max(entries.shape))
    beside = index_at[:main_axis] + [(index_at[main_axis] + 1) % entries.shape[main_axis]] + index_at[main_axis + 1:]
    return entries.at[tuple(index_at)].set(least).at[tuple(beside)].set(top_value)


def shard_levels(own_key, extent, split, low, high):
    def one(dim, parts):
        heights = jax.random.uniform(jax.random.fold_in(jax.random.fold_in(own_key, 6), dim), (parts,), jnp.float32, low / len(split), high / len(split))
        return jnp.repeat(jnp.exp(heights), extent[dim] // parts).reshape((-1,) + (1,) * (len(extent) - dim - 1))

    gain = one(*split[0])
    for cut in split[1:]:
        gain = gain * one(*cut)
    return gain


def bell_draw(key, extent, width, reach, pieces=(), dtype=jnp.bfloat16):
    loudness = shard_levels(key, extent, pieces, -0.22, 0.18) if pieces else 1.0
    values = jax.random.normal(key, extent, jnp.float32) * width * loudness
    return jnp.minimum(jnp.maximum(values, -reach), reach).astype(dtype)


def setup_inputs(seed: int = 0) -> dict:
    key_of = jax.random.split(jax.random.key(seed), 7)
    return {
        "latents": bell_draw(key_of[0], (TOKENS, D), 1.0, 6.0, ((0, 64), (1, 4))),
        "noise": bell_draw(key_of[1], (TOKENS, D), 1.0, 6.0, ((0, 64), (1, 4))),
        "timesteps": plant(jax.random.randint(key_of[2], (CLIPS,), 0, STEPS), jax.random.fold_in(key_of[2], 1), 0, STEPS - 1).astype(jnp.int32),
        "qkv_weight": bell_draw(key_of[3], (D, 4, N_SEQ, 3, 2 * HQ * HDIM), D ** -0.5, 0.078125, ((0, 8), (1, 4), (2, 8))),
        "qk_gain": jnp.clip(1.0 + 0.1 * jax.random.normal(key_of[4], (2, 2, HDIM), jnp.float32), 0.5, 1.5),
        "fake_cotangent": bell_draw(key_of[5], (TOKENS, 2, N_SEQ, 2 * HQ * HDIM), 1.0, 6.0, ((0, 8), (2, 8))),
    }


flow_shift = 5.0
norm_eps = 1e-06
scale_eps = 1e-05

def noise_level(timestep):
    fraction = (timestep.astype(jnp.float32) + 1.0) / STEPS
    return flow_shift * fraction / (1.0 + (flow_shift - 1.0) * fraction)

def head_norm(values_in, norm_gain):
    return values_in * lax.rsqrt(lax.optimization_barrier(jnp.mean(values_in * values_in, axis=-1, keepdims=True)) + norm_eps) * norm_gain

def reference(latents, noise, timesteps, qkv_weight, qk_gain, fake_cotangent):
    clip_len = TOK_DEV * N_SEQ
    head_cols = 2 * HQ * HDIM
    latent_clips = latents.reshape(N_DP, clip_len, D)
    noise_clips = noise.reshape(N_DP, clip_len, D)
    cotangent = fake_cotangent.reshape(N_DP, clip_len, 2, N_SEQ, 2 * HQ, HDIM)
    flat_weight = qkv_weight.reshape(D, 4 * N_SEQ * 3 * head_cols)
    slot_gains = jnp.stack([qk_gain[0], qk_gain[0], qk_gain[1], qk_gain[1]])

    def one_clip(running, inputs):
        latent_clip, noise_clip, timestep, clip_cotangent = inputs
        level = noise_level(timestep)
        noised = (1.0 - level) * latent_clip.astype(jnp.float32) + level * noise_clip.astype(jnp.float32)
        row_mean = lax.optimization_barrier(jnp.sum(noised, 1, keepdims=True)) / D
        row_var = lax.optimization_barrier(jnp.sum(noised * noised, 1, keepdims=True)) / D - row_mean * row_mean
        normed = ((noised - row_mean) * lax.rsqrt(row_var + norm_eps)).astype(jnp.bfloat16)
        projected = jnp.dot(normed, flat_weight, preferred_element_type=jnp.float32)
        projected = projected.reshape(clip_len, 4, N_SEQ, 3, 2 * HQ, HDIM)
        query_heads = head_norm(projected[:, :, :, 0], slot_gains[None, :, None, None, 0, :]).astype(jnp.bfloat16)
        key_heads = head_norm(projected[:, :, :, 1], slot_gains[None, :, None, None, 1, :]).astype(jnp.bfloat16)
        value_heads = projected[:, :, :, 2].astype(jnp.bfloat16)
        scores = jnp.einsum('qrshd,krshd->rshqk', query_heads.astype(jnp.float32), key_heads.astype(jnp.float32)) / math.sqrt(HDIM)
        exponent = jnp.exp(scores)
        softmax_out = (exponent / lax.optimization_barrier(jnp.sum(exponent, -1, keepdims=True))).astype(jnp.bfloat16)
        head_out = jnp.einsum('rshqk,krshd->qrshd', softmax_out.astype(jnp.float32), value_heads.astype(jnp.float32)).astype(jnp.bfloat16)
        real_out = head_out[:, 0:2].astype(jnp.float32)
        fake_out = head_out[:, 2:4].astype(jnp.float32)
        clip_mean = jnp.mean(jnp.abs(real_out))
        score_gap = (fake_out - real_out) / (clip_mean + scale_eps)
        score_gap = score_gap.reshape(clip_len, 2, N_SEQ, 2, HQ, HDIM).transpose(0, 3, 1, 2, 4, 5)
        score_gap = score_gap.reshape(clip_len, 4 * N_SEQ * HQ * HDIM).astype(jnp.bfloat16)
        value_step = jnp.einsum('bshqk,qbshd->kbshd', softmax_out[2:4].astype(jnp.float32), clip_cotangent.astype(jnp.float32)).astype(jnp.bfloat16)
        running = running + jnp.dot(normed.T, value_step.reshape(clip_len, 2 * N_SEQ * head_cols), preferred_element_type=jnp.float32)
        return (running, score_gap)
    zero_grad = jnp.zeros((D, 2 * N_SEQ * head_cols), jnp.float32)
    weight_grad, dmd_rows = lax.scan(one_clip, zero_grad, (latent_clips, noise_clips, timesteps, cotangent))
    weight_grad = weight_grad.reshape(2, D // 2, 2, N_SEQ, head_cols).transpose(0, 2, 1, 3, 4)
    weight_grad = weight_grad.reshape(4, D // 2, N_SEQ, head_cols)
    return (dmd_rows.reshape(N_DP * clip_len, 4 * N_SEQ * HQ * HDIM), weight_grad)
```

```python
import math

import jax
import jax.numpy as jnp
from jax import lax
from jax.sharding import PartitionSpec as P

HDIM = 128
STEPS = 1000


flow_shift = 5.0
norm_eps = 1e-06
scale_eps = 1e-05

BF16 = jnp.bfloat16
F32 = jnp.float32


def noise_level(timestep):
    fraction = (timestep.astype(F32) + 1.0) / STEPS
    return flow_shift * fraction / (1.0 + (flow_shift - 1.0) * fraction)


def head_norm(values_in, norm_gain):
    return (
        values_in
        * lax.rsqrt(jnp.mean(values_in * values_in, axis=-1, keepdims=True) + norm_eps)
        * norm_gain
    )


def x_ring(block):
    route = []
    for r in range(4):
        for d in range(8):
            to = (r + (1 if d % 2 == 0 else -1)) % 4
            route.append((r * 8 + d, to * 8 + d))
    return lax.ppermute(block, ("role", "dp"), route)


def y_ring(block):
    route = []
    for d in range(8):
        for s in range(8):
            to = (s + (2 if d % 2 == 0 else -2)) % 8
            route.append((d * 8 + s, d * 8 + to))
    return lax.ppermute(block, ("dp", "seq"), route)


def z_ring(block):
    route = []
    for d in range(8):
        to = (d + (2 if d % 2 == 0 else -2)) % 8
        route.append((d, to))
    return lax.ppermute(block, "dp", route)


def x_up(block, hop):
    return lax.ppermute(block, "role", [(r, (r + hop) % 4) for r in range(4)])


def y_up(block, hop):
    return lax.ppermute(block, "seq", [(s, (s + 2 * hop) % 8) for s in range(8)])


def core_swap(block):
    return lax.ppermute(block, "dp", [(d, d ^ 1) for d in range(8)])


def zlo_swap(block):
    return lax.ppermute(block, "seq", [(s, s ^ 1) for s in range(8)])


def model_swap(block):
    return lax.ppermute(block, "role", [(r, r ^ 2) for r in range(4)])


def z_step(block, steps):
    return lax.ppermute(block, "dp", [(d, (d + 2 * steps) % 8) for d in range(8)])


def body(latents, noise, timesteps, qkv_weight, qk_gain, fake_cotangent):
    role = lax.axis_index("role")
    dp = lax.axis_index("dp")
    seq = lax.axis_index("seq")
    model = role // 2
    group = role % 2
    core = dp % 2
    z_hi = dp // 2
    y = seq // 2
    z_lo = seq % 2
    way = 1 - 2 * core

    tok, quarter = latents.shape
    width = 4 * quarter
    half = tok // 2
    rows = qkv_weight.shape[0]
    cols = 3 * HDIM

    w = qkv_weight[:, 0, 0]
    keep = lax.dynamic_slice_in_dim(w, model * HDIM, HDIM, 2).reshape(rows, cols)
    give = lax.dynamic_slice_in_dim(w, (1 - model) * HDIM, HDIM, 2).reshape(rows, cols)

    fence = lax.optimization_barrier

    def after(value, other):
        return fence((value, other))[0]

    level = noise_level(timesteps[0])
    noised = (1.0 - level) * latents.astype(F32) + level * noise.astype(F32)
    sums = jnp.stack([jnp.sum(noised, 1), jnp.sum(noised * noised, 1)])
    parts = [lax.ppermute(sums, "role", [(r, r ^ hop) for r in range(4)]) for hop in (1, 2, 3)]
    other = model_swap(give)
    totals = sums + parts[0] + parts[1] + parts[2]
    row_mean = totals[0] / width
    row_var = totals[1] / width - row_mean * row_mean
    normed = ((noised - row_mean[:, None]) * lax.rsqrt(row_var + norm_eps)[:, None]).astype(BF16)
    beside = zlo_swap(normed)
    first = jnp.where(z_lo == 0, normed, beside).reshape(2, half, quarter)
    second = jnp.where(z_lo == 0, beside, normed).reshape(2, half, quarter)
    own_a = jnp.stack([first[0], second[0]])
    own_b = jnp.stack([first[1], second[1]])

    mine = [jnp.concatenate([keep, other], axis=1)]
    own_a, own_b, mine[0] = fence((own_a, own_b, mine[0]))
    for step in range(3):
        mine.append(z_ring(mine[-1]))

    a_lo, a_hi, b_lo, b_hi = x_up(own_a, 1), x_up(own_a, -1), y_up(own_b, 1), y_up(own_b, -1)
    a_op = x_ring(jnp.where(core == 0, a_lo, a_hi))
    b_op = y_ring(jnp.where(core == 0, b_lo, b_hi))
    block_a = jnp.zeros((2, half, width), BF16)
    for off, got in ((0, own_a), (3, a_lo), (1, a_hi), (2, a_op)):
        block_a = lax.dynamic_update_slice(block_a, got, (0, 0, ((role + off) % 4) * quarter))
    block_b = jnp.zeros((4, 2, half, quarter), BF16)
    for off, got in ((0, own_b), (3, b_lo), (1, b_hi), (2, b_op)):
        block_b = lax.dynamic_update_slice(block_b, got[None], ((y + off) % 4, 0, 0, 0))
    a_lo, a_hi, b_lo, b_hi = y_up(block_a, 1), y_up(block_a, -1), x_up(block_b, 1), x_up(block_b, -1)
    on_a = jnp.where(core == 0, a_lo, a_hi)
    on_b = jnp.where(core == 0, b_lo, b_hi)
    a_op = y_ring(on_a)
    b_op = x_ring(on_b)

    mine = [after(piece, (on_a, on_b)) for piece in mine]
    theirs = [core_swap(after(piece, a_op)) for piece in mine]
    weight = jnp.zeros((8 * rows, 2 * cols), BF16)
    for step in range(4):
        src = (z_hi - way * step) % 4
        weight = lax.dynamic_update_slice(weight, mine[step], ((src * 2 + core) * rows, 0))
    for step in range(4):
        src = (z_hi + way * step) % 4
        weight = lax.dynamic_update_slice(weight, theirs[step], ((src * 2 + 1 - core) * rows, 0))

    tokens = jnp.zeros((4, 2, 2, half, width), BF16)
    from_a = ((0, after(block_a, block_b)), (3, a_lo), (1, a_hi), (2, a_op))
    from_b = ((0, block_b), (3, b_lo), (1, b_hi), (2, b_op))
    for (off, got_a), (_, got_b) in zip(from_a, from_b):
        tokens = lax.dynamic_update_slice(
            tokens, got_a[None, :, None], ((y + off) % 4, 0, 0, 0, 0)
        )
        tokens = lax.dynamic_update_slice(
            tokens, got_b[:, :, None], (0, 0, 1, 0, ((role + off) % 4) * quarter)
        )
    clip_len = 8 * tok
    tokens = tokens.reshape(clip_len, width)
    own_gain = lax.dynamic_index_in_dim(qk_gain, model, 0, keepdims=False)
    other_gain = lax.dynamic_index_in_dim(qk_gain, 1 - model, 0, keepdims=False)
    projected = jnp.dot(tokens, weight, preferred_element_type=F32)
    projected = projected.reshape(clip_len, 2, 3, HDIM)
    gains = jnp.stack([own_gain, other_gain])
    query = head_norm(projected[:, :, 0], gains[None, :, 0]).astype(BF16)
    key = head_norm(projected[:, :, 1], gains[None, :, 1]).astype(BF16)
    value = projected[:, :, 2].astype(BF16)
    scores = jnp.einsum("qhd,khd->hqk", query, key, preferred_element_type=F32) / math.sqrt(HDIM)
    exponent = jnp.exp(scores)
    probs = (exponent / jnp.sum(exponent, -1, keepdims=True)).astype(BF16)

    cotangent = lax.dynamic_slice(
        fake_cotangent, (0, group, 0, model * HDIM), (clip_len, 1, 1, HDIM)
    ).reshape(clip_len, HDIM)
    fake_probs = lax.dynamic_index_in_dim(probs, 1 - model, 0, keepdims=False)
    value_step = lax.dot_general(
        fake_probs, cotangent, (((0,), (0,)), ((), ())), preferred_element_type=F32
    ).astype(BF16)
    grad = lax.dot_general(
        tokens, value_step, (((0,), (0,)), ((), ())), preferred_element_type=F32
    ).astype(BF16)
    height = width // 16
    grad = grad.reshape(2, 4, 2, height, HDIM)
    to_sibling = lax.dynamic_index_in_dim(grad, 1 - core, 2, keepdims=False)
    from_sibling = core_swap(to_sibling)
    stay = lax.dynamic_index_in_dim(grad, core, 2, keepdims=False)
    head_out = jnp.einsum("hqk,khd->hqd", probs, value, preferred_element_type=F32).astype(BF16)
    head_out = head_out.astype(F32)
    real_out = jnp.where(model == 0, head_out[0], head_out[1])
    fake_out = jnp.where(model == 0, head_out[1], head_out[0])
    gap = (fake_out - real_out).astype(BF16)
    own_sum = jnp.broadcast_to(jnp.sum(jnp.abs(real_out)), (1, HDIM))
    role_sum = after(own_sum, from_sibling)
    for hop in (1, 2):
        role_sum = role_sum + lax.ppermute(role_sum, "role", [(r, r ^ hop) for r in range(4)])
    high = lax.reduce_precision(role_sum, 8, 7)
    middle = lax.reduce_precision(role_sum - high, 8, 7)
    low = role_sum - high - middle
    tail_rows = jnp.pad(jnp.concatenate([high, middle, low]), ((0, 13), (0, 0))).astype(BF16)
    message = jnp.concatenate(
        [gap.reshape(8, tok, HDIM), jnp.broadcast_to(tail_rows, (8, 16, HDIM))], axis=1
    )
    message = lax.all_to_all(message, "seq", split_axis=0, concat_axis=0, tiled=True)

    pair_sum = (stay.astype(F32) + from_sibling.astype(F32)).astype(BF16)
    total = lax.dynamic_index_in_dim(pair_sum, z_hi, 1, keepdims=False).astype(F32)
    for step in (1, 2, 3):
        leaving = lax.dynamic_index_in_dim(pair_sum, (z_hi + step) % 4, 1, keepdims=False)
        total = total + z_step(leaving, step).astype(F32)
    grad_keep = lax.dynamic_index_in_dim(total, model, 0, keepdims=False)
    grad_give = lax.dynamic_index_in_dim(total, 1 - model, 0, keepdims=False)
    grad_got = model_swap(grad_give.astype(BF16)).astype(F32)
    scale_sum = jnp.sum(message[:, tok : tok + 3, 0].astype(F32))
    clip_mean = scale_sum / (clip_len * 32 * HDIM)
    gap_rows = message[:, :tok].transpose(1, 0, 2).reshape(tok, 8 * HDIM)
    dmd_rows = (gap_rows.astype(F32) / (clip_mean + scale_eps)).astype(BF16)
    grad_out = jnp.concatenate(
        [
            jnp.where(model == 0, grad_keep, grad_got),
            jnp.where(model == 0, grad_got, grad_keep),
        ],
        axis=1,
    )

    return (dmd_rows, grad_out.reshape(1, height, 1, 2 * HDIM))


def solution(mesh):
    placed = (
        P(("dp", "seq"), "role"),
        P(("dp", "seq"), "role"),
        P("dp"),
        P("dp", "role", "seq", None, None),
        P(),
        P("dp", None, "seq", None),
    )
    return jax.shard_map(
        body,
        mesh=mesh,
        in_specs=placed,
        out_specs=(P(("dp", "seq"), "role"), P("role", "dp", "seq", None)),
        check_vma=False,
    )
```

```python
import math

import jax
import jax.numpy as jnp
from jax import lax
from jax.sharding import PartitionSpec as P

HDIM = 128
STEPS = 1000


flow_shift = 5.0
norm_eps = 1e-06
scale_eps = 1e-05

BF16 = jnp.bfloat16
F32 = jnp.float32


def noise_level(timestep):
    fraction = (timestep.astype(F32) + 1.0) / STEPS
    return flow_shift * fraction / (1.0 + (flow_shift - 1.0) * fraction)


def head_norm(values_in, norm_gain):
    return (
        values_in
        * lax.rsqrt(jnp.mean(values_in * values_in, axis=-1, keepdims=True) + norm_eps)
        * norm_gain
    )


def x_ring(block):
    route = []
    for r in range(4):
        for d in range(8):
            to = (r + (1 if d % 2 == 0 else -1)) % 4
            route.append((r * 8 + d, to * 8 + d))
    return lax.ppermute(block, ("role", "dp"), route)


def y_ring(block):
    route = []
    for d in range(8):
        for s in range(8):
            to = (s + (2 if d % 2 == 0 else -2)) % 8
            route.append((d * 8 + s, d * 8 + to))
    return lax.ppermute(block, ("dp", "seq"), route)


def z_ring(block):
    route = []
    for d in range(8):
        to = (d + (2 if d % 2 == 0 else -2)) % 8
        route.append((d, to))
    return lax.ppermute(block, "dp", route)


def x_up(block, hop):
    return lax.ppermute(block, "role", [(r, (r + hop) % 4) for r in range(4)])


def y_up(block, hop):
    return lax.ppermute(block, "seq", [(s, (s + 2 * hop) % 8) for s in range(8)])


def z_back(block):
    route = []
    for d in range(8):
        to = (d + (-2 if d % 2 == 0 else 2)) % 8
        route.append((d, to))
    return lax.ppermute(block, "dp", route)


def core_swap(block):
    return lax.ppermute(block, "dp", [(d, d ^ 1) for d in range(8)])


def zlo_swap(block):
    return lax.ppermute(block, "seq", [(s, s ^ 1) for s in range(8)])


def model_swap(block):
    return lax.ppermute(block, "role", [(r, r ^ 2) for r in range(4)])


def z_step(block, steps):
    return lax.ppermute(block, "dp", [(d, (d + 2 * steps) % 8) for d in range(8)])


def body(latents, noise, timesteps, qkv_weight, qk_gain, fake_cotangent):
    role = lax.axis_index("role")
    dp = lax.axis_index("dp")
    seq = lax.axis_index("seq")
    model = role // 2
    group = role % 2
    core = dp % 2
    z_hi = dp // 2
    y = seq // 2
    z_lo = seq % 2
    way = 1 - 2 * core

    tok, quarter = latents.shape
    width = 4 * quarter
    half = tok // 2
    rows = qkv_weight.shape[0]
    cols = 3 * HDIM

    w = qkv_weight[:, 0, 0]
    keep = lax.dynamic_slice_in_dim(w, model * HDIM, HDIM, 2).reshape(rows, cols)
    give = lax.dynamic_slice_in_dim(w, (1 - model) * HDIM, HDIM, 2).reshape(rows, cols)

    fence = lax.optimization_barrier

    def after(value, other):
        return fence((value, other))[0]

    level = noise_level(timesteps[0])
    noised = (1.0 - level) * latents.astype(F32) + level * noise.astype(F32)
    sums = jnp.stack([jnp.sum(noised, 1), jnp.sum(noised * noised, 1)])
    parts = [lax.ppermute(sums, "role", [(r, r ^ hop) for r in range(4)]) for hop in (1, 2, 3)]
    other = model_swap(give)
    totals = sums + parts[0] + parts[1] + parts[2]
    row_mean = totals[0] / width
    row_var = totals[1] / width - row_mean * row_mean
    normed = ((noised - row_mean[:, None]) * lax.rsqrt(row_var + norm_eps)[:, None]).astype(BF16)
    beside = zlo_swap(normed)
    first = jnp.where(z_lo == 0, normed, beside).reshape(2, half, quarter)
    second = jnp.where(z_lo == 0, beside, normed).reshape(2, half, quarter)
    mine = [jnp.concatenate([keep, other], axis=1)]
    first, second, mine[0] = fence((first, second, mine[0]))
    mine.append(z_ring(mine[0]))
    mine.append(z_ring(mine[1]))
    mine.append(z_back(mine[0]))
    own_a = jnp.stack([first[0], second[0]])
    own_b = jnp.stack([first[1], second[1]])

    a_lo, a_hi, b_lo, b_hi = x_up(own_a, 1), x_up(own_a, -1), y_up(own_b, 1), y_up(own_b, -1)
    a_op = x_ring(jnp.where(core == 0, a_lo, a_hi))
    b_op = y_ring(jnp.where(core == 0, b_lo, b_hi))
    block_a = jnp.zeros((2, half, width), BF16)
    for off, got in ((0, own_a), (3, a_lo), (1, a_hi), (2, a_op)):
        block_a = lax.dynamic_update_slice(block_a, got, (0, 0, ((role + off) % 4) * quarter))
    block_b = jnp.zeros((4, 2, half, quarter), BF16)
    for off, got in ((0, own_b), (3, b_lo), (1, b_hi), (2, b_op)):
        block_b = lax.dynamic_update_slice(block_b, got[None], ((y + off) % 4, 0, 0, 0))
    a_lo, a_hi, b_lo, b_hi = y_up(block_a, 1), y_up(block_a, -1), x_up(block_b, 1), x_up(block_b, -1)
    on_a = jnp.where(core == 0, a_lo, a_hi)
    on_b = jnp.where(core == 0, b_lo, b_hi)
    a_op = y_ring(on_a)
    b_op = x_ring(on_b)

    mine = [after(piece, (on_a, on_b)) for piece in mine]
    theirs = [core_swap(after(piece, a_op)) for piece in mine]
    weight = jnp.zeros((8 * rows, 2 * cols), BF16)
    for step in range(4):
        src = (z_hi - way * step) % 4
        weight = lax.dynamic_update_slice(weight, mine[step], ((src * 2 + core) * rows, 0))
    for step in range(4):
        src = (z_hi + way * step) % 4
        weight = lax.dynamic_update_slice(weight, theirs[step], ((src * 2 + 1 - core) * rows, 0))

    tokens = jnp.zeros((4, 2, 2, half, width), BF16)
    from_a = ((0, after(block_a, block_b)), (3, a_lo), (1, a_hi), (2, a_op))
    from_b = ((0, block_b), (3, b_lo), (1, b_hi), (2, b_op))
    for (off, got_a), (_, got_b) in zip(from_a, from_b):
        tokens = lax.dynamic_update_slice(
            tokens, got_a[None, :, None], ((y + off) % 4, 0, 0, 0, 0)
        )
        tokens = lax.dynamic_update_slice(
            tokens, got_b[:, :, None], (0, 0, 1, 0, ((role + off) % 4) * quarter)
        )
    clip_len = 8 * tok
    tokens = tokens.reshape(clip_len, width)
    own_gain = lax.dynamic_index_in_dim(qk_gain, model, 0, keepdims=False)
    other_gain = lax.dynamic_index_in_dim(qk_gain, 1 - model, 0, keepdims=False)
    projected = jnp.dot(tokens, weight, preferred_element_type=F32)
    projected = projected.reshape(clip_len, 2, 3, HDIM)
    gains = jnp.stack([own_gain, other_gain])
    query = head_norm(projected[:, :, 0], gains[None, :, 0]).astype(BF16)
    key = head_norm(projected[:, :, 1], gains[None, :, 1]).astype(BF16)
    value = projected[:, :, 2].astype(BF16)
    scores = jnp.einsum("qhd,khd->hqk", query, key, preferred_element_type=F32) / math.sqrt(HDIM)
    exponent = jnp.exp(scores)
    probs = (exponent / jnp.sum(exponent, -1, keepdims=True)).astype(BF16)

    cotangent = lax.dynamic_slice(
        fake_cotangent, (0, group, 0, model * HDIM), (clip_len, 1, 1, HDIM)
    ).reshape(clip_len, HDIM)
    fake_probs = lax.dynamic_index_in_dim(probs, 1 - model, 0, keepdims=False)
    value_step = lax.dot_general(
        fake_probs, cotangent, (((0,), (0,)), ((), ())), preferred_element_type=F32
    ).astype(BF16)
    grad = lax.dot_general(
        tokens, value_step, (((0,), (0,)), ((), ())), preferred_element_type=F32
    ).astype(BF16)
    height = width // 16
    grad = grad.reshape(2, 4, 2, height, HDIM)
    to_sibling = lax.dynamic_index_in_dim(grad, 1 - core, 2, keepdims=False)
    from_sibling = core_swap(to_sibling)
    stay = lax.dynamic_index_in_dim(grad, core, 2, keepdims=False)
    head_out = jnp.einsum("hqk,khd->hqd", probs, value, preferred_element_type=F32).astype(BF16)
    head_out = head_out.astype(F32)
    real_out = jnp.where(model == 0, head_out[0], head_out[1])
    fake_out = jnp.where(model == 0, head_out[1], head_out[0])
    gap = (fake_out - real_out).astype(BF16)
    own_sum = jnp.broadcast_to(jnp.sum(jnp.abs(real_out)), (1, HDIM))
    role_sum = after(own_sum, from_sibling)
    for hop in (1, 2):
        role_sum = role_sum + lax.ppermute(role_sum, "role", [(r, r ^ hop) for r in range(4)])
    high = lax.reduce_precision(role_sum, 8, 7)
    middle = lax.reduce_precision(role_sum - high, 8, 7)
    low = role_sum - high - middle
    tail_rows = jnp.pad(jnp.concatenate([high, middle, low]), ((0, 13), (0, 0))).astype(BF16)
    message = jnp.concatenate(
        [gap.reshape(8, tok, HDIM), jnp.broadcast_to(tail_rows, (8, 16, HDIM))], axis=1
    )
    message = lax.all_to_all(message, "seq", split_axis=0, concat_axis=0, tiled=True)

    pair_sum = (stay.astype(F32) + from_sibling.astype(F32)).astype(BF16)
    total = lax.dynamic_index_in_dim(pair_sum, z_hi, 1, keepdims=False).astype(F32)
    for step in (1, 2, 3):
        leaving = lax.dynamic_index_in_dim(pair_sum, (z_hi + step) % 4, 1, keepdims=False)
        total = total + z_step(leaving, step).astype(F32)
    grad_keep = lax.dynamic_index_in_dim(total, model, 0, keepdims=False)
    grad_give = lax.dynamic_index_in_dim(total, 1 - model, 0, keepdims=False)
    scale_sum = jnp.sum(message[:, tok : tok + 3, 0].astype(F32))
    clip_mean = scale_sum / (clip_len * 32 * HDIM)
    gap_rows = message[:, :tok].transpose(1, 0, 2).reshape(tok, 8 * HDIM)
    dmd_rows = (gap_rows.astype(F32) / (clip_mean + scale_eps)).astype(BF16)
    grad_give = after(grad_give, dmd_rows)
    grad_got = model_swap(grad_give.astype(BF16)).astype(F32)
    grad_out = jnp.concatenate(
        [
            jnp.where(model == 0, grad_keep, grad_got),
            jnp.where(model == 0, grad_got, grad_keep),
        ],
        axis=1,
    )

    return (dmd_rows, grad_out.reshape(1, height, 1, 2 * HDIM))


def solution(mesh):
    placed = (
        P(("dp", "seq"), "role"),
        P(("dp", "seq"), "role"),
        P("dp"),
        P("dp", "role", "seq", None, None),
        P(),
        P("dp", None, "seq", None),
    )
    return jax.shard_map(
        body,
        mesh=mesh,
        in_specs=placed,
        out_specs=(P(("dp", "seq"), "role"), P("role", "dp", "seq", None)),
        check_vma=False,
    )
```

```python
import math

import jax
import jax.numpy as jnp
from jax import lax
from jax.sharding import PartitionSpec as P

HDIM = 128
STEPS = 1000


flow_shift = 5.0
norm_eps = 1e-06
scale_eps = 1e-05

BF16 = jnp.bfloat16
F32 = jnp.float32


def noise_level(timestep):
    fraction = (timestep.astype(F32) + 1.0) / STEPS
    return flow_shift * fraction / (1.0 + (flow_shift - 1.0) * fraction)


def head_norm(values_in, norm_gain):
    return (
        values_in
        * lax.rsqrt(jnp.mean(values_in * values_in, axis=-1, keepdims=True) + norm_eps)
        * norm_gain
    )


def x_ring(block):
    route = []
    for r in range(4):
        for d in range(8):
            to = (r + (1 if d % 2 == 0 else -1)) % 4
            route.append((r * 8 + d, to * 8 + d))
    return lax.ppermute(block, ("role", "dp"), route)


def y_ring(block):
    route = []
    for d in range(8):
        for s in range(8):
            to = (s + (2 if d % 2 == 0 else -2)) % 8
            route.append((d * 8 + s, d * 8 + to))
    return lax.ppermute(block, ("dp", "seq"), route)


def z_ring(block):
    route = []
    for d in range(8):
        to = (d + (2 if d % 2 == 0 else -2)) % 8
        route.append((d, to))
    return lax.ppermute(block, "dp", route)


def x_up(block, hop):
    return lax.ppermute(block, "role", [(r, (r + hop) % 4) for r in range(4)])


def y_up(block, hop):
    return lax.ppermute(block, "seq", [(s, (s + 2 * hop) % 8) for s in range(8)])


def core_swap(block):
    return lax.ppermute(block, "dp", [(d, d ^ 1) for d in range(8)])


def zlo_swap(block):
    return lax.ppermute(block, "seq", [(s, s ^ 1) for s in range(8)])


def model_swap(block):
    return lax.ppermute(block, "role", [(r, r ^ 2) for r in range(4)])


def z_step(block, steps):
    return lax.ppermute(block, "dp", [(d, (d + 2 * steps) % 8) for d in range(8)])


def body(latents, noise, timesteps, qkv_weight, qk_gain, fake_cotangent):
    role = lax.axis_index("role")
    dp = lax.axis_index("dp")
    seq = lax.axis_index("seq")
    model = role // 2
    group = role % 2
    core = dp % 2
    z_hi = dp // 2
    y = seq // 2
    z_lo = seq % 2
    way = 1 - 2 * core

    tok, quarter = latents.shape
    width = 4 * quarter
    half = tok // 2
    rows = qkv_weight.shape[0]
    cols = 3 * HDIM

    w = qkv_weight[:, 0, 0]
    keep = lax.dynamic_slice_in_dim(w, model * HDIM, HDIM, 2).reshape(rows, cols)
    give = lax.dynamic_slice_in_dim(w, (1 - model) * HDIM, HDIM, 2).reshape(rows, cols)

    fence = lax.optimization_barrier

    def after(value, other):
        return fence((value, other))[0]

    level = noise_level(timesteps[0])
    noised = (1.0 - level) * latents.astype(F32) + level * noise.astype(F32)
    sums = jnp.stack([jnp.sum(noised, 1), jnp.sum(noised * noised, 1)])
    parts = [lax.ppermute(sums, "role", [(r, r ^ hop) for r in range(4)]) for hop in (1, 2, 3)]
    other = model_swap(give)
    totals = sums + parts[0] + parts[1] + parts[2]
    row_mean = totals[0] / width
    row_var = totals[1] / width - row_mean * row_mean
    normed = ((noised - row_mean[:, None]) * lax.rsqrt(row_var + norm_eps)[:, None]).astype(BF16)
    beside = zlo_swap(normed)
    first = jnp.where(z_lo == 0, normed, beside).reshape(2, half, quarter)
    second = jnp.where(z_lo == 0, beside, normed).reshape(2, half, quarter)
    own_a = jnp.stack([first[0], second[0]])
    own_b = jnp.stack([first[1], second[1]])

    mine = [jnp.concatenate([keep, other], axis=1)]
    own_a, own_b, mine[0] = fence((own_a, own_b, mine[0]))
    for step in range(3):
        mine.append(z_ring(mine[-1]))

    a_lo, a_hi, b_lo, b_hi = x_up(own_a, 1), x_up(own_a, -1), y_up(own_b, 1), y_up(own_b, -1)
    a_op = x_ring(jnp.where(core == 0, a_lo, a_hi))
    b_op = y_ring(jnp.where(core == 0, b_lo, b_hi))
    block_a = jnp.zeros((2, half, width), BF16)
    for off, got in ((0, own_a), (3, a_lo), (1, a_hi), (2, a_op)):
        block_a = lax.dynamic_update_slice(block_a, got, (0, 0, ((role + off) % 4) * quarter))
    block_b = jnp.zeros((4, 2, half, quarter), BF16)
    for off, got in ((0, own_b), (3, b_lo), (1, b_hi), (2, b_op)):
        block_b = lax.dynamic_update_slice(block_b, got[None], ((y + off) % 4, 0, 0, 0))
    a_lo, a_hi, b_lo, b_hi = y_up(block_a, 1), y_up(block_a, -1), x_up(block_b, 1), x_up(block_b, -1)
    on_a = jnp.where(core == 0, a_lo, a_hi)
    on_b = jnp.where(core == 0, b_lo, b_hi)
    a_op = y_ring(on_a)
    b_op = x_ring(on_b)

    mine = [after(piece, (on_a, on_b)) for piece in mine]
    theirs = [core_swap(after(piece, a_op)) for piece in mine]
    weight = jnp.zeros((8 * rows, 2 * cols), BF16)
    for step in range(4):
        src = (z_hi - way * step) % 4
        weight = lax.dynamic_update_slice(weight, mine[step], ((src * 2 + core) * rows, 0))
    for step in range(4):
        src = (z_hi + way * step) % 4
        weight = lax.dynamic_update_slice(weight, theirs[step], ((src * 2 + 1 - core) * rows, 0))

    tokens = jnp.zeros((4, 2, 2, half, width), BF16)
    from_a = ((0, after(block_a, block_b)), (3, a_lo), (1, a_hi), (2, a_op))
    from_b = ((0, block_b), (3, b_lo), (1, b_hi), (2, b_op))
    for (off, got_a), (_, got_b) in zip(from_a, from_b):
        tokens = lax.dynamic_update_slice(
            tokens, got_a[None, :, None], ((y + off) % 4, 0, 0, 0, 0)
        )
        tokens = lax.dynamic_update_slice(
            tokens, got_b[:, :, None], (0, 0, 1, 0, ((role + off) % 4) * quarter)
        )
    clip_len = 8 * tok
    tokens = tokens.reshape(clip_len, width)
    own_gain = lax.dynamic_index_in_dim(qk_gain, model, 0, keepdims=False)
    other_gain = lax.dynamic_index_in_dim(qk_gain, 1 - model, 0, keepdims=False)
    projected = jnp.dot(tokens, weight, preferred_element_type=F32)
    projected = projected.reshape(clip_len, 2, 3, HDIM)
    gains = jnp.stack([own_gain, other_gain])
    query = head_norm(projected[:, :, 0], gains[None, :, 0]).astype(BF16)
    key = head_norm(projected[:, :, 1], gains[None, :, 1]).astype(BF16)
    value = projected[:, :, 2].astype(BF16)
    scores = jnp.einsum("qhd,khd->hqk", query, key, preferred_element_type=F32) / math.sqrt(HDIM)
    exponent = jnp.exp(scores)
    probs = (exponent / jnp.sum(exponent, -1, keepdims=True)).astype(BF16)

    cotangent = lax.dynamic_slice(
        fake_cotangent, (0, group, 0, model * HDIM), (clip_len, 1, 1, HDIM)
    ).reshape(clip_len, HDIM)
    fake_probs = lax.dynamic_index_in_dim(probs, 1 - model, 0, keepdims=False)
    value_step = lax.dot_general(
        fake_probs, cotangent, (((0,), (0,)), ((), ())), preferred_element_type=F32
    ).astype(BF16)
    grad = lax.dot_general(
        tokens, value_step, (((0,), (0,)), ((), ())), preferred_element_type=F32
    ).astype(BF16)
    height = width // 16
    grad = grad.reshape(2, 4, 2, height, HDIM)
    to_sibling = lax.dynamic_index_in_dim(grad, 1 - core, 2, keepdims=False)
    from_sibling = core_swap(to_sibling)
    stay = lax.dynamic_index_in_dim(grad, core, 2, keepdims=False)
    head_out = jnp.einsum("hqk,khd->hqd", probs, value, preferred_element_type=F32).astype(BF16)
    head_out = head_out.astype(F32)
    real_out = jnp.where(model == 0, head_out[0], head_out[1])
    fake_out = jnp.where(model == 0, head_out[1], head_out[0])
    gap = (fake_out - real_out).astype(BF16)
    own_sum = jnp.broadcast_to(jnp.sum(jnp.abs(real_out)), (1, HDIM))
    part_sum = after(own_sum, from_sibling)
    high = lax.reduce_precision(part_sum, 8, 7)
    middle = lax.reduce_precision(part_sum - high, 8, 7)
    low = part_sum - high - middle
    tail_rows = jnp.pad(jnp.concatenate([high, middle, low]), ((0, 13), (0, 0))).astype(BF16)
    message = jnp.concatenate(
        [gap.reshape(8, tok, HDIM), jnp.broadcast_to(tail_rows, (8, 16, HDIM))], axis=1
    )
    message = lax.all_to_all(message, "seq", split_axis=0, concat_axis=0, tiled=True)

    pair_sum = (stay.astype(F32) + from_sibling.astype(F32)).astype(BF16)
    total = lax.dynamic_index_in_dim(pair_sum, z_hi, 1, keepdims=False).astype(F32)
    for step in (1, 2, 3):
        leaving = lax.dynamic_index_in_dim(pair_sum, (z_hi + step) % 4, 1, keepdims=False)
        total = total + z_step(leaving, step).astype(F32)
    grad_keep = lax.dynamic_index_in_dim(total, model, 0, keepdims=False)
    grad_give = lax.dynamic_index_in_dim(total, 1 - model, 0, keepdims=False)
    grad_got = model_swap(grad_give.astype(BF16)).astype(F32)
    role_sum = jnp.sum(message[:, tok : tok + 3].astype(F32), axis=(0, 1)).reshape(1, HDIM)
    hops = [lax.ppermute(role_sum, "role", [(r, r ^ hop) for r in range(4)]) for hop in (1, 2, 3)]
    scale_sum = (role_sum + hops[0] + hops[1] + hops[2])[0, 0]
    clip_mean = scale_sum / (clip_len * 32 * HDIM)
    gap_rows = message[:, :tok].transpose(1, 0, 2).reshape(tok, 8 * HDIM)
    dmd_rows = (gap_rows.astype(F32) / (clip_mean + scale_eps)).astype(BF16)
    grad_got = after(grad_got, dmd_rows)
    grad_out = jnp.concatenate(
        [
            jnp.where(model == 0, grad_keep, grad_got),
            jnp.where(model == 0, grad_got, grad_keep),
        ],
        axis=1,
    )

    return (dmd_rows, grad_out.reshape(1, height, 1, 2 * HDIM))


def solution(mesh):
    placed = (
        P(("dp", "seq"), "role"),
        P(("dp", "seq"), "role"),
        P("dp"),
        P("dp", "role", "seq", None, None),
        P(),
        P("dp", None, "seq", None),
    )
    return jax.shard_map(
        body,
        mesh=mesh,
        in_specs=placed,
        out_specs=(P(("dp", "seq"), "role"), P("role", "dp", "seq", None)),
        check_vma=False,
    )
```

```python
import math

import jax
import jax.numpy as jnp
from jax import lax
from jax.sharding import PartitionSpec as P

HDIM = 128
STEPS = 1000


flow_shift = 5.0
norm_eps = 1e-06
scale_eps = 1e-05

BF16 = jnp.bfloat16
F32 = jnp.float32


def noise_level(timestep):
    fraction = (timestep.astype(F32) + 1.0) / STEPS
    return flow_shift * fraction / (1.0 + (flow_shift - 1.0) * fraction)


def head_norm(values_in, norm_gain):
    return (
        values_in
        * lax.rsqrt(jnp.mean(values_in * values_in, axis=-1, keepdims=True) + norm_eps)
        * norm_gain
    )


def x_ring(block):
    route = []
    for r in range(4):
        for d in range(8):
            to = (r + (1 if d % 2 == 0 else -1)) % 4
            route.append((r * 8 + d, to * 8 + d))
    return lax.ppermute(block, ("role", "dp"), route)


def y_ring(block):
    route = []
    for d in range(8):
        for s in range(8):
            to = (s + (2 if d % 2 == 0 else -2)) % 8
            route.append((d * 8 + s, d * 8 + to))
    return lax.ppermute(block, ("dp", "seq"), route)


def z_ring(block):
    route = []
    for d in range(8):
        to = (d + (2 if d % 2 == 0 else -2)) % 8
        route.append((d, to))
    return lax.ppermute(block, "dp", route)


def x_up(block, hop):
    return lax.ppermute(block, "role", [(r, (r + hop) % 4) for r in range(4)])


def y_up(block, hop):
    return lax.ppermute(block, "seq", [(s, (s + 2 * hop) % 8) for s in range(8)])


def core_swap(block):
    return lax.ppermute(block, "dp", [(d, d ^ 1) for d in range(8)])


def zlo_swap(block):
    return lax.ppermute(block, "seq", [(s, s ^ 1) for s in range(8)])


def model_swap(block):
    return lax.ppermute(block, "role", [(r, r ^ 2) for r in range(4)])


def z_step(block, steps):
    return lax.ppermute(block, "dp", [(d, (d + 2 * steps) % 8) for d in range(8)])


def body(latents, noise, timesteps, qkv_weight, qk_gain, fake_cotangent):
    role = lax.axis_index("role")
    dp = lax.axis_index("dp")
    seq = lax.axis_index("seq")
    model = role // 2
    group = role % 2
    core = dp % 2
    z_hi = dp // 2
    y = seq // 2
    z_lo = seq % 2
    way = 1 - 2 * core

    tok, quarter = latents.shape
    width = 4 * quarter
    half = tok // 2
    rows = qkv_weight.shape[0]
    cols = 3 * HDIM

    w = qkv_weight[:, 0, 0]
    keep = lax.dynamic_slice_in_dim(w, model * HDIM, HDIM, 2).reshape(rows, cols)
    give = lax.dynamic_slice_in_dim(w, (1 - model) * HDIM, HDIM, 2).reshape(rows, cols)

    fence = lax.optimization_barrier

    def after(value, other):
        return fence((value, other))[0]

    level = noise_level(timesteps[0])
    noised = (1.0 - level) * latents.astype(F32) + level * noise.astype(F32)
    sums = jnp.stack([jnp.sum(noised, 1), jnp.sum(noised * noised, 1)])
    parts = [lax.ppermute(sums, "role", [(r, r ^ hop) for r in range(4)]) for hop in (1, 2, 3)]
    other = model_swap(give)
    totals = sums + parts[0] + parts[1] + parts[2]
    row_mean = totals[0] / width
    row_var = totals[1] / width - row_mean * row_mean
    normed = ((noised - row_mean[:, None]) * lax.rsqrt(row_var + norm_eps)[:, None]).astype(BF16)
    beside = zlo_swap(normed)
    first = jnp.where(z_lo == 0, normed, beside).reshape(2, half, quarter)
    second = jnp.where(z_lo == 0, beside, normed).reshape(2, half, quarter)
    own_a = jnp.stack([first[0], second[0]])
    own_b = jnp.stack([first[1], second[1]])

    mine = [jnp.concatenate([keep, other], axis=1)]
    weight = jnp.zeros((8 * rows, 2 * cols), BF16)
    weight = lax.dynamic_update_slice(weight, mine[0], ((z_hi * 2 + core) * rows, 0))
    own_a, own_b, weight = fence((own_a, own_b, weight))
    for step in range(3):
        mine.append(z_ring(mine[-1]))

    a_lo, a_hi, b_lo, b_hi = x_up(own_a, 1), x_up(own_a, -1), y_up(own_b, 1), y_up(own_b, -1)
    a_op = x_ring(jnp.where(core == 0, a_lo, a_hi))
    b_op = y_ring(jnp.where(core == 0, b_lo, b_hi))
    block_a = jnp.zeros((2, half, width), BF16)
    for off, got in ((0, own_a), (3, a_lo), (1, a_hi), (2, a_op)):
        block_a = lax.dynamic_update_slice(block_a, got, (0, 0, ((role + off) % 4) * quarter))
    block_b = jnp.zeros((4, 2, half, quarter), BF16)
    for off, got in ((0, own_b), (3, b_lo), (1, b_hi), (2, b_op)):
        block_b = lax.dynamic_update_slice(block_b, got[None], ((y + off) % 4, 0, 0, 0))
    a_lo, a_hi, b_lo, b_hi = y_up(block_a, 1), y_up(block_a, -1), x_up(block_b, 1), x_up(block_b, -1)
    on_a = jnp.where(core == 0, a_lo, a_hi)
    on_b = jnp.where(core == 0, b_lo, b_hi)
    a_op = y_ring(on_a)
    b_op = x_ring(on_b)

    mine = [after(piece, (on_a, on_b)) for piece in mine]
    theirs = [core_swap(after(piece, a_op)) for piece in mine]
    for step in range(1, 4):
        src = (z_hi - way * step) % 4
        weight = lax.dynamic_update_slice(weight, mine[step], ((src * 2 + core) * rows, 0))
    for step in range(4):
        src = (z_hi + way * step) % 4
        weight = lax.dynamic_update_slice(weight, theirs[step], ((src * 2 + 1 - core) * rows, 0))

    tokens = jnp.zeros((4, 2, 2, half, width), BF16)
    from_a = ((0, after(block_a, block_b)), (3, a_lo), (1, a_hi), (2, a_op))
    from_b = ((0, block_b), (3, b_lo), (1, b_hi), (2, b_op))
    for (off, got_a), (_, got_b) in zip(from_a, from_b):
        tokens = lax.dynamic_update_slice(
            tokens, got_a[None, :, None], ((y + off) % 4, 0, 0, 0, 0)
        )
        tokens = lax.dynamic_update_slice(
            tokens, got_b[:, :, None], (0, 0, 1, 0, ((role + off) % 4) * quarter)
        )
    clip_len = 8 * tok
    tokens = tokens.reshape(clip_len, width)
    own_gain = lax.dynamic_index_in_dim(qk_gain, model, 0, keepdims=False)
    other_gain = lax.dynamic_index_in_dim(qk_gain, 1 - model, 0, keepdims=False)
    projected = jnp.dot(tokens, weight, preferred_element_type=F32)
    projected = projected.reshape(clip_len, 2, 3, HDIM)
    gains = jnp.stack([own_gain, other_gain])
    query = head_norm(projected[:, :, 0], gains[None, :, 0]).astype(BF16)
    key = head_norm(projected[:, :, 1], gains[None, :, 1]).astype(BF16)
    value = projected[:, :, 2].astype(BF16)
    scores = jnp.einsum("qhd,khd->hqk", query, key, preferred_element_type=F32) / math.sqrt(HDIM)
    exponent = jnp.exp(scores)
    probs = (exponent / jnp.sum(exponent, -1, keepdims=True)).astype(BF16)

    cotangent = lax.dynamic_slice(
        fake_cotangent, (0, group, 0, model * HDIM), (clip_len, 1, 1, HDIM)
    ).reshape(clip_len, HDIM)
    fake_probs = lax.dynamic_index_in_dim(probs, 1 - model, 0, keepdims=False)
    value_step = lax.dot_general(
        fake_probs, cotangent, (((0,), (0,)), ((), ())), preferred_element_type=F32
    ).astype(BF16)
    grad = lax.dot_general(
        tokens, value_step, (((0,), (0,)), ((), ())), preferred_element_type=F32
    ).astype(BF16)
    height = width // 16
    grad = grad.reshape(2, 4, 2, height, HDIM)
    to_sibling = lax.dynamic_index_in_dim(grad, 1 - core, 2, keepdims=False)
    from_sibling = core_swap(to_sibling)
    stay = lax.dynamic_index_in_dim(grad, core, 2, keepdims=False)
    head_out = jnp.einsum("hqk,khd->hqd", probs, value, preferred_element_type=F32).astype(BF16)
    head_out = head_out.astype(F32)
    real_out = jnp.where(model == 0, head_out[0], head_out[1])
    fake_out = jnp.where(model == 0, head_out[1], head_out[0])
    gap = (fake_out - real_out).astype(BF16)
    own_sum = jnp.broadcast_to(jnp.sum(jnp.abs(real_out)), (1, HDIM))
    part_sum = after(own_sum, from_sibling)
    high = lax.reduce_precision(part_sum, 8, 7)
    middle = lax.reduce_precision(part_sum - high, 8, 7)
    low = part_sum - high - middle
    tail_rows = jnp.pad(jnp.concatenate([high, middle, low]), ((0, 13), (0, 0))).astype(BF16)
    message = jnp.concatenate(
        [gap.reshape(8, tok, HDIM), jnp.broadcast_to(tail_rows, (8, 16, HDIM))], axis=1
    )
    message = lax.all_to_all(message, "seq", split_axis=0, concat_axis=0, tiled=True)

    pair_sum = (stay.astype(F32) + from_sibling.astype(F32)).astype(BF16)
    total = lax.dynamic_index_in_dim(pair_sum, z_hi, 1, keepdims=False).astype(F32)
    for step in (1, 2, 3):
        leaving = lax.dynamic_index_in_dim(pair_sum, (z_hi + step) % 4, 1, keepdims=False)
        total = total + z_step(leaving, step).astype(F32)
    grad_keep = lax.dynamic_index_in_dim(total, model, 0, keepdims=False)
    grad_give = lax.dynamic_index_in_dim(total, 1 - model, 0, keepdims=False)
    grad_got = model_swap(grad_give.astype(BF16)).astype(F32)
    role_sum = jnp.sum(message[:, tok : tok + 3].astype(F32), axis=(0, 1)).reshape(1, HDIM)
    hops = [lax.ppermute(role_sum, "role", [(r, r ^ hop) for r in range(4)]) for hop in (1, 2, 3)]
    scale_sum = (role_sum + hops[0] + hops[1] + hops[2])[0, 0]
    clip_mean = scale_sum / (clip_len * 32 * HDIM)
    gap_rows = message[:, :tok].transpose(1, 0, 2).reshape(tok, 8 * HDIM)
    dmd_rows = (gap_rows.astype(F32) / (clip_mean + scale_eps)).astype(BF16)
    grad_got = after(grad_got, dmd_rows)
    grad_out = jnp.concatenate(
        [
            jnp.where(model == 0, grad_keep, grad_got),
            jnp.where(model == 0, grad_got, grad_keep),
        ],
        axis=1,
    )

    return (dmd_rows, grad_out.reshape(1, height, 1, 2 * HDIM))


def solution(mesh):
    placed = (
        P(("dp", "seq"), "role"),
        P(("dp", "seq"), "role"),
        P("dp"),
        P("dp", "role", "seq", None, None),
        P(),
        P("dp", None, "seq", None),
    )
    return jax.shard_map(
        body,
        mesh=mesh,
        in_specs=placed,
        out_specs=(P(("dp", "seq"), "role"), P("role", "dp", "seq", None)),
        check_vma=False,
    )
```
